32 devices in a mesh: qx: 8 (over y, x, core), qy: 4 (over z).
Axes of the slice: x: 2, y: 2, z: 4, core: 2. Of those that a mesh axis runs over, the one named last changes fastest.
Arguments:
- image_tiles: bfloat16 [8, 4, 256, 64, 128], P('qx', 'qy'), may hold values from -6 to 6
- observed: bfloat16 [8, 4, 256, 64, 128], P('qx', 'qy'), may hold values from -6 to 6
- phases: float32 [8, 4, 256, 64, 128], P('qx', 'qy'), may hold values from -3.140625 to 3.140625
- interpolate: bfloat16 [64, 64], replicated, may hold values from -0.75 to 0.75
- local_weights: bfloat16 [8, 4, 2, 4, 4, 64, 64], P('qx', 'qy'), may hold values from -0.375 to 0.375
- merge_weights: bfloat16 [8, 4, 2, 4, 4, 64, 64], P('qx', 'qy'), may hold values from -0.375 to 0.375
- output_weight: bfloat16 [64, 64], replicated, may hold values from -0.75 to 0.75
Outputs:
- gradient: bfloat16 [8, 4, 256, 64, 128], P('qx', 'qy')
The draws below stay inside these ranges and needn't reach their ends.
All inputs are finite; a program needn't handle non-finite values.
Results may differ from the reference program's by a relative error of at most 0.02.
Values may be sent and summed in bfloat16 or wider, within the bound.
No kernel may reach another device: no remote copies, remote signals or barrier semaphores. Data moves between devices by JAX's collectives and lax.ppermute only.
A program may use at most 128 MiB of HBM per device.

```python
import jax
import jax.numpy as jnp
from jax import lax

R = 64
L = 128
GROUPS = 256
LOCAL = 2
DIST = 2
N_QX = 8
N_QY = 4


def block_scale(stream_key, extent, shards, smallest, largest):
    gain = 1.0
    for dim, shards_of in shards:
        heights = jax.random.uniform(jax.random.fold_in(jax.random.fold_in(stream_key, 6), dim), (shards_of,), jnp.float32, smallest / len(shards), largest / len(shards))
        gain = gain * jnp.repeat(jnp.exp(heights), extent[dim] // shards_of).reshape((-1,) + (1,) * (len(extent) - 1 - dim))
    return gain


def normal_values(rng, shape, deviation, bound, cuts=(), kind=jnp.bfloat16):
    level = block_scale(rng, shape, cuts, -0.22, 0.18) if cuts else 1.0
    values = jax.random.normal(rng, shape, jnp.float32) * deviation * level
    return jnp.minimum(jnp.maximum(values, -bound), bound).astype(kind)


def setup_inputs(seed: int = 0) -> dict:
    streams_of = jax.random.split(jax.random.key(seed), 8)
    image_tiles = normal_values(streams_of[0], (N_QX, N_QY, GROUPS, R, L), 1.0, 6.0, ((0, 8), (1, 4)))
    observed = normal_values(streams_of[1], (N_QX, N_QY, GROUPS, R, L), 1.0, 6.0, ((0, 8), (1, 4)))
    phases = jnp.clip(jax.random.uniform(streams_of[2], (N_QX, N_QY, GROUPS, R, L), jnp.float32, -3.140625, 3.140625), -3.140625, 3.140625)
    interpolate = normal_values(streams_of[3], (R, R), R ** -0.5, 0.75)
    local_weights = normal_values(streams_of[4], (N_QX, N_QY, LOCAL, 4, 4, R, R), (4 * R) ** -0.5, 0.375, ((0, 8), (1, 4)))
    merge_weights = normal_values(streams_of[5], (N_QX, N_QY, DIST, 4, 4, R, R), (4 * R) ** -0.5, 0.375, ((0, 8), (1, 4)))
    output_weight = normal_values(streams_of[6], (R, R), R ** -0.5, 0.75)
    return dict(image_tiles=image_tiles, observed=observed, phases=phases, interpolate=interpolate, local_weights=local_weights, merge_weights=merge_weights, output_weight=output_weight)


def mixing(weight, data, form):
    return jnp.einsum(form, weight.astype(jnp.float32), data.astype(jnp.float32)).astype(jnp.bfloat16)


def level_bit(axis_count, level_index, depth):
    total_bits = axis_count.bit_length() - 1
    return (level_index * (total_bits - 1)) // max(depth - 1, 1)


def route_all(field, level_index):
    stride_x = 2 ** level_bit(N_QX, level_index, DIST)
    stride_y = 2 ** level_bit(N_QY, level_index, DIST)
    outer_x = N_QX // (2 * stride_x)
    outer_y = N_QY // (2 * stride_y)
    quarter_size = GROUPS // 4
    split_field = field.reshape(outer_x, 2, stride_x, outer_y, 2, stride_y, 2, 2, quarter_size, R, L)
    moved = jnp.transpose(split_field, (0, 6, 2, 3, 7, 5, 1, 4, 8, 9, 10))
    return moved.reshape(N_QX * N_QY, 4, quarter_size, R, L)


def reference(image_tiles, observed, phases, interpolate, local_weights, merge_weights, output_weight):
    device_count = N_QX * N_QY
    quarter_size = GROUPS // 4
    blocks = image_tiles.reshape(device_count, GROUPS, R, L)
    levels = local_weights.reshape(device_count, LOCAL, 4, 4, R, R)
    merges = merge_weights.reshape(device_count, DIST, 4, 4, R, R)

    def forward_local(packed):
        tiles, weights = packed
        current = mixing(interpolate, tiles, "op,gpl->gol")
        for section_index in range(LOCAL):
            stride_size = 4 ** section_index
            blocked = current.reshape(GROUPS // (4 * stride_size), 4, stride_size, R, L)
            current = mixing(weights[section_index], blocked, "kcor,acbrl->akbol").reshape(GROUPS, R, L)
        return current

    def merge_forward(packed):
        weight, pieces = packed
        return mixing(weight, pieces, "scor,chrl->shol")

    def merge_adjoint(packed):
        weight, pieces = packed
        return mixing(weight, pieces, "scor,shol->chrl")

    current = lax.map(forward_local, (blocks, levels)).reshape(N_QX, N_QY, GROUPS, R, L)
    for level_index in range(DIST):
        pieces = route_all(current, level_index)
        current = lax.map(merge_forward, (merges[:, level_index], pieces))
        current = current.reshape(N_QX, N_QY, GROUPS, R, L)
    merged_y = current

    cas_wave = jnp.cos(phases) + jnp.sin(phases)
    predicted = jnp.einsum("or,tvgrl->tvgol", output_weight.astype(jnp.float32), merged_y.astype(jnp.float32))
    residual = (cas_wave * predicted - observed.astype(jnp.float32)).astype(jnp.bfloat16)
    weighted = (cas_wave * residual.astype(jnp.float32)).astype(jnp.bfloat16)
    back = mixing(output_weight, weighted, "or,tvgol->tvgrl")

    for level_index in reversed(range(DIST)):
        pieces = back.reshape(device_count, 4, quarter_size, R, L)
        terms = lax.map(merge_adjoint, (merges[:, level_index], pieces))
        terms = terms.reshape(N_QX, N_QY, GROUPS, R, L)
        back = route_all(terms, level_index).reshape(N_QX, N_QY, GROUPS, R, L)

    def adjoint_local(packed):
        current, weights = packed
        for section_index in reversed(range(LOCAL)):
            stride_size = 4 ** section_index
            blocked = current.reshape(GROUPS // (4 * stride_size), 4, stride_size, R, L)
            current = mixing(weights[section_index], blocked, "kcor,akbol->acbrl").reshape(GROUPS, R, L)
        return mixing(interpolate, current, "op,gol->gpl")

    gradient = lax.map(adjoint_local, (back.reshape(device_count, GROUPS, R, L), levels))
    return gradient.reshape(N_QX, N_QY, GROUPS, R, L)
```

```python
import functools

import jax
import jax.numpy as jnp
import numpy as np
from jax import lax
from jax.experimental import pallas as pl
from jax.experimental.pallas import tpu as pltpu
from jax.sharding import PartitionSpec as P

PIECES = ((4, 12), (16,), (16,), (12, 4))
ROOT2 = float(np.sqrt(2.0))
QUARTER_PI = float(np.pi / 4)
INV_PI = float(1.0 / np.pi)
PI_HIGH = 3.140625
PI_MID = float(np.float32(np.pi - 3.140625))
PI_LOW = float(np.pi - 3.140625 - float(np.float32(np.pi - 3.140625)))


def level_bit(axis_count, level_index, depth):
    total_bits = axis_count.bit_length() - 1
    return level_index * (total_bits - 1) // max(depth - 1, 1)


def dot(a, b):
    return jnp.dot(a, b, preferred_element_type=jnp.float32)


def cas(angle):
    turns = jnp.floor(angle * INV_PI + 0.75)
    rest = ((angle - turns * PI_HIGH) - turns * PI_MID) - turns * PI_LOW + QUARTER_PI
    square = rest * rest
    poly = jnp.float32(-2.5052108e-8)
    for c in (2.7557319e-6, -1.9841270e-4, 8.3333333e-3, -1.6666667e-1, 1.0):
        poly = poly * square + jnp.float32(c)
    half = turns * 0.5
    odd = half - jnp.floor(half)
    sign = ROOT2 - (4.0 * ROOT2) * odd
    return poly * rest * sign


def stacked(columns):
    return jnp.concatenate([jnp.concatenate(row, axis=1) for row in columns], axis=0)


def tile(y, i, j, r, n):
    return y[i * r : (i + 1) * r, j * n : (j + 1) * n]


def prep_local_kernel(lw_ref, ip_ref, w0_ref, w1_ref, w0t_ref, w1t_ref):
    r = ip_ref.shape[0]
    ip = ip_ref[...]
    for k in range(4):
        rows = pl.ds(k * r, r)
        for c in range(4):
            cols = pl.ds(c * r, r)
            a = dot(lw_ref[0, k, c], ip)
            b = lw_ref[1, k, c]
            w0_ref[rows, cols] = a.astype(jnp.bfloat16)
            w1_ref[rows, cols] = b
            w0t_ref[cols, rows] = a.T.astype(jnp.bfloat16)
            w1t_ref[cols, rows] = b.astype(jnp.float32).T.astype(jnp.bfloat16)


def prep_merge_kernel(bits_ref, mw_ref, ow_ref, a_ref, at_ref, b_ref, bt_ref):
    r = ow_ref.shape[0]
    ow = ow_ref[...]
    k0, k1 = bits_ref[0], bits_ref[1]
    for s in range(4):
        rows = pl.ds(s * r, r)
        for c in range(4):
            cols = pl.ds(c * r, r)
            a = mw_ref[0, k1 ^ s, k0 ^ c]
            b = dot(ow, mw_ref[1, s, k1 ^ c])
            a_ref[rows, cols] = a
            at_ref[cols, rows] = a.astype(jnp.float32).T.astype(jnp.bfloat16)
            b_ref[rows, cols] = b.astype(jnp.bfloat16)
            bt_ref[cols, rows] = b.T.astype(jnp.bfloat16)


def forward_local_kernel(sizes, bits_ref, image_ref, w0_ref, w1_ref, *outs):
    r, n = image_ref.shape[-2:]
    w0, w1 = w0_ref[...], w1_ref[...]
    for d in range(4):
        q = bits_ref[0] ^ d
        x = stacked([[image_ref[q, 0, 4 * a + c] for a in range(4)] for c in range(4)])
        y = dot(w0, x).astype(jnp.bfloat16)
        x = stacked([[tile(y, e, a, r, n) for e in range(4)] for a in range(4)])
        y = dot(w1, x).astype(jnp.bfloat16)
        start = 0
        for piece, size in enumerate(sizes):
            for h in range(size):
                a, e = divmod(start + h, 4)
                outs[4 * piece + d][h] = tile(y, a, e, r, n)
            start += size


def adjoint_local_kernel(sizes, bits_ref, w0t_ref, w1t_ref, *refs):
    ins, out_ref = refs[: 4 * len(sizes)], refs[-1]
    r, n = out_ref.shape[-2:]
    w0t, w1t = w0t_ref[...], w1t_ref[...]
    places = [(piece, h) for piece, size in enumerate(sizes) for h in range(size)]
    for d in range(4):
        q = bits_ref[0] ^ d

        def piece_of(a, e):
            piece, h = places[4 * a + e]
            return ins[4 * piece + d][h]

        x = stacked([[piece_of(a, e) for e in range(4)] for a in range(4)])
        y = dot(w1t, x).astype(jnp.bfloat16)
        x = stacked([[tile(y, a, e, r, n) for a in range(4)] for e in range(4)])
        y = dot(w0t, x).astype(jnp.bfloat16)
        for a in range(4):
            for c in range(4):
                out_ref[q, 0, 4 * a + c] = tile(y, c, a, r, n)


def merge_kernel(w_ref, *refs):
    ins, outs = refs[:4], refs[4:]
    size, r, n = ins[0].shape
    w = w_ref[...]
    for i in range(0, size, 4):
        x = stacked([[ref[i + j] for j in range(4)] for ref in ins])
        y = dot(w, x).astype(jnp.bfloat16)
        for d in range(4):
            for j in range(4):
                outs[d][i + j] = tile(y, d, j, r, n)


def residual_kernel(b_ref, bt_ref, phases_ref, observed_ref, *refs):
    ins, outs = refs[:4], refs[4:]
    size, r, n = ins[0].shape
    x = stacked([[ref[j] for j in range(size)] for ref in ins])
    predicted = dot(b_ref[...], x)
    weighted = []
    for s in range(4):
        row = []
        for j in range(size):
            wave = cas(phases_ref[s, j])
            residual = wave * tile(predicted, s, j, r, n) - observed_ref[s, j].astype(jnp.float32)
            residual = residual.astype(jnp.bfloat16).astype(jnp.float32)
            row.append((wave * residual).astype(jnp.bfloat16))
        weighted.append(row)
    y = dot(bt_ref[...], stacked(weighted)).astype(jnp.bfloat16)
    for d in range(4):
        for j in range(size):
            outs[d][j] = tile(y, d, j, r, n)


SMEM = pl.BlockSpec(memory_space=pltpu.SMEM)
VMEM = pl.BlockSpec(memory_space=pltpu.VMEM)
PARAMS = pltpu.CompilerParams(vmem_limit_bytes=40 * 2**20)


def cost(levels, columns, byte_count):
    return pl.CostEstimate(
        flops=levels * 2 * 256 * 256 * columns, bytes_accessed=byte_count, transcendentals=0
    )


def exchange(blocks, mask_x, mask_y):
    count_x, count_y = lax.axis_size("qx"), lax.axis_size("qy")
    along_y = [(s, s ^ mask_y) for s in range(count_y)]
    along_x = [(s, s ^ mask_x) for s in range(count_x)]
    both = [
        (x * count_y + y, (x ^ mask_x) * count_y + (y ^ mask_y))
        for x in range(count_x)
        for y in range(count_y)
    ]
    return (
        blocks[0],
        lax.ppermute(blocks[1], "qy", along_y),
        lax.ppermute(blocks[2], "qx", along_x),
        lax.ppermute(blocks[3], ("qx", "qy"), both),
    )


def local(image_tiles, observed, phases, interpolate, local_weights, merge_weights, output_weight):
    groups, r, n = image_tiles.shape[2:]
    depth = merge_weights.shape[2]
    chunks = len(PIECES)
    quarter = groups // 4
    chunk = quarter // chunks
    bf16 = jnp.bfloat16
    box = r * n * 2

    masks, own = [], []
    for level in range(depth):
        bit_x = level_bit(lax.axis_size("qx"), level, depth)
        bit_y = level_bit(lax.axis_size("qy"), level, depth)
        masks.append((2**bit_x, 2**bit_y))
        own.append(
            2 * (jnp.right_shift(lax.axis_index("qx"), bit_x) & 1)
            + (jnp.right_shift(lax.axis_index("qy"), bit_y) & 1)
        )
    bits = jnp.stack(own).astype(jnp.int32)
    square = jax.ShapeDtypeStruct((4 * r, 4 * r), bf16)

    with jax.named_scope("prep_local"):
        w0, w1, w0t, w1t = pl.pallas_call(
            prep_local_kernel,
            out_shape=[square] * 4,
            in_specs=[VMEM] * 2,
            out_specs=[VMEM] * 4,
            cost_estimate=cost(0, 0, 10 * 4 * r * 4 * r),
        )(local_weights[0, 0], interpolate)
    with jax.named_scope("prep_merge"):
        m0, m0t, m1, m1t = pl.pallas_call(
            prep_merge_kernel,
            out_shape=[square] * 4,
            in_specs=[SMEM, VMEM, VMEM],
            out_specs=[VMEM] * 4,
            cost_estimate=cost(0, 0, 10 * 4 * r * 4 * r),
        )(bits, merge_weights[0, 0], output_weight)

    image = image_tiles.reshape(4, chunks, chunk, r, n)
    phase4 = phases.reshape(4, quarter, r, n)
    observed4 = observed.reshape(4, quarter, r, n)

    def merge(weight, blocks):
        size = blocks[0].shape[0]
        return pl.pallas_call(
            merge_kernel,
            out_shape=[jax.ShapeDtypeStruct((size, r, n), bf16)] * 4,
            in_specs=[VMEM] * 5,
            out_specs=[VMEM] * 4,
            compiler_params=PARAMS,
            cost_estimate=cost(1, size * n, 8 * size * box),
        )(weight, *blocks)

    def through_data(blocks, start):
        size = blocks[0].shape[0]
        step = 4
        small = pl.BlockSpec((step, r, n), lambda i: (i, 0, 0))
        large = pl.BlockSpec((4, step, r, n), lambda i: (0, start // step + i, 0, 0))
        whole = pl.BlockSpec((4 * r, 4 * r), lambda i: (0, 0))
        return pl.pallas_call(
            residual_kernel,
            grid=(size // step,),
            out_shape=[jax.ShapeDtypeStruct((size, r, n), bf16)] * 4,
            in_specs=[whole, whole, large, large] + [small] * 4,
            out_specs=[small] * 4,
            compiler_params=PARAMS,
            cost_estimate=cost(6, size * n, 20 * size * box),
        )(m1, m1t, phase4, observed4, *blocks)

    pieces = []
    for index, sizes in enumerate(PIECES):
        with jax.named_scope(f"local_forward_{index}"):
            outs = pl.pallas_call(
                functools.partial(forward_local_kernel, sizes),
                grid=(1,),
                out_shape=[
                    jax.ShapeDtypeStruct((size, r, n), bf16) for size in sizes for _ in range(4)
                ],
                in_specs=[
                    SMEM,
                    pl.BlockSpec((4, 1, chunk, r, n), lambda i, index=index: (0, index, 0, 0, 0)),
                    pl.BlockSpec((4 * r, 4 * r), lambda i: (0, 0)),
                    pl.BlockSpec((4 * r, 4 * r), lambda i: (0, 0)),
                ],
                out_specs=[
                    pl.BlockSpec((size, r, n), lambda i: (0, 0, 0))
                    for size in sizes
                    for _ in range(4)
                ],
                compiler_params=PARAMS,
                cost_estimate=cost(2, chunk * n, 8 * chunk * box),
            )(bits, image, w0, w1)
        start = index * chunk
        for piece, size in enumerate(sizes):
            pieces.append((index, start, outs[4 * piece : 4 * piece + 4]))
            start += size

    returned = [[] for _ in PIECES]
    for index, start, blocks in pieces:
        with jax.named_scope(f"merges_{start}"):
            blocks = exchange(blocks, *masks[0])
            blocks = merge(m0, blocks)
            blocks = exchange(blocks, *masks[1])
            blocks = through_data(blocks, start)
            blocks = exchange(blocks, *masks[1])
            blocks = merge(m0t, blocks)
            returned[index].extend(exchange(blocks, *masks[0]))

    gradient = None
    for index, sizes in enumerate(PIECES):
        with jax.named_scope(f"local_adjoint_{index}"):
            blocks = returned[index]
            operands = [bits, w0t, w1t, *blocks]
            in_specs = [
                SMEM,
                pl.BlockSpec((4 * r, 4 * r), lambda i: (0, 0)),
                pl.BlockSpec((4 * r, 4 * r), lambda i: (0, 0)),
            ] + [pl.BlockSpec(b.shape, lambda i: (0, 0, 0)) for b in blocks]
            aliases = {}
            if gradient is not None:
                aliases = {len(operands): 0}
                operands.append(gradient)
                in_specs.append(pl.BlockSpec(memory_space=pl.ANY))
            gradient = pl.pallas_call(
                functools.partial(adjoint_local_kernel, sizes),
                grid=(1,),
                out_shape=jax.ShapeDtypeStruct((4, chunks, chunk, r, n), bf16),
                in_specs=in_specs,
                out_specs=pl.BlockSpec(
                    (4, 1, chunk, r, n), lambda i, index=index: (0, index, 0, 0, 0)
                ),
                input_output_aliases=aliases,
                compiler_params=PARAMS,
                cost_estimate=cost(2, chunk * n, 8 * chunk * box),
            )(*operands)
    return gradient.reshape(1, 1, groups, r, n)


def solution(mesh):
    split = P("qx", "qy", None, None, None)
    weights = P("qx", "qy", None, None, None, None, None)
    return jax.shard_map(
        local,
        mesh=mesh,
        in_specs=(split, split, split, P(), weights, weights, P()),
        out_specs=split,
        check_vma=False,
    )
```

```python
import functools

import jax
import jax.numpy as jnp
import numpy as np
from jax import lax
from jax.experimental import pallas as pl
from jax.experimental.pallas import tpu as pltpu
from jax.sharding import PartitionSpec as P

PIECES = ((16,), (16,), (16,), (16,))
ACTIONS = (
    ".K10_", "+X00d", "+X00x", "+X00z", ".K13_", "+X03x", ".K12_", "+X02x", ".K11_", ".PM0_",
    "-X00d", "+X01x", "-X00x", "+X01z", "-X00z", ".X10_", "+X10d", "-X03x", "+X01d", "-X02x",
    "+X10x", "-X01x", "+X10z", "-X01z", "-X10d", "-X01d", ".X11_", "+X11d", "+X02z", "-X10x",
    "-X10z", ".Y10_", "+Y10x", "+X11x", "+X11z", "-X11d", "+Y10z", "-X02z", "+X02d", ".PA0_",
    "-Y10x", "+Y10d", "-X11x", "+X03z", "-X11z", ".Y11_", "+Y11d", "-Y10z", "+Y11x", "-X02d",
    ".X12_", "+X12x", "-Y10d", "+X12z", "-X03z", "+X03d", ".Y00_", "-Y11d", "+X12d", "-Y11x",
    "+Y00z", "-X12x", "+Y00d", "-X12z", "+Y11z", "-X03d", ".X13_", "+X13d", "-X12d", ".Y12_",
    "+Y12d", "-Y00z", "+X13x", "-Y00d", "+Y00x", "-Y11z", ".Y01_", "+Y01d", "-X13d", "+X13z",
    "-Y12d", "+Y01x", "-X13x", "+Y12x", "-Y00x", "+Y01z", "-Y01d", "+Y12z", ".K50_", "-X13z",
    ".Y13_", "+Y13x", "-Y01x", "+Y13d", "-Y12x", "+Y13z", "-Y01z", ".K51_", "-Y12z", ".Y02_",
    "+Y02z", "+Y02d", "-Y13x", "+Y02x", "-Y13d", "-Y13z", ".Y03_", "+Y03d", "+Y03x", "-Y02z",
    "+Y03z", "-Y02d", "-Y02x", ".K52_", "-Y03d", "-Y03x", "-Y03z", ".K53_",
)
VMEM_GRANT = 16 * 2**20
TOKEN = jax.ShapeDtypeStruct((8, 128), jnp.float32)
ROOT2 = float(np.sqrt(2.0))
QUARTER_PI = float(np.pi / 4)
INV_PI = float(1.0 / np.pi)
PI_HIGH = 3.140625
PI_MID = float(np.float32(np.pi - 3.140625))
PI_LOW = float(np.pi - 3.140625 - float(np.float32(np.pi - 3.140625)))


def level_bit(axis_count, level_index, depth):
    total_bits = axis_count.bit_length() - 1
    return level_index * (total_bits - 1) // max(depth - 1, 1)


def dot(a, b):
    return jnp.dot(a, b, preferred_element_type=jnp.float32)


def cas(angle):
    turns = jnp.floor(angle * INV_PI + 0.75)
    rest = ((angle - turns * PI_HIGH) - turns * PI_MID) - turns * PI_LOW + QUARTER_PI
    square = rest * rest
    poly = jnp.float32(-2.5052108e-8)
    for c in (2.7557319e-6, -1.9841270e-4, 8.3333333e-3, -1.6666667e-1, 1.0):
        poly = poly * square + jnp.float32(c)
    half = turns * 0.5
    odd = half - jnp.floor(half)
    sign = ROOT2 - (4.0 * ROOT2) * odd
    return poly * rest * sign


def stacked(columns):
    return jnp.concatenate([jnp.concatenate(row, axis=1) for row in columns], axis=0)


def tile(y, i, j, r, n):
    return y[i * r : (i + 1) * r, j * n : (j + 1) * n]


def own_index(masks):
    x, y = lax.axis_index("qx"), lax.axis_index("qy")
    return [
        2 * jnp.where(x & mask_x != 0, 1, 0) + jnp.where(y & mask_y != 0, 1, 0)
        for mask_x, mask_y in masks
    ]


def blocks_of(stack, r):
    return [
        jnp.concatenate([stack[4 * k + c] for c in range(4)], axis=1) for k in range(4)
    ]


def prep_adjoint_kernel(lw_ref, ip_ref, *refs):
    r = ip_ref.shape[0]
    w0t_ref, w1t_ref = refs[-3:-1]
    ip = ip_ref[...]
    for k in range(4):
        cols = pl.ds(k * r, r)
        for c in range(4):
            rows = pl.ds(c * r, r)
            w0t_ref[rows, cols] = dot(lw_ref[0, k, c], ip).T.astype(jnp.bfloat16)
            w1t_ref[rows, cols] = lw_ref[1, k, c].astype(jnp.float32).T.astype(jnp.bfloat16)


def prep_merge_kernel(masks, mw_ref, ow_ref, *refs):
    r = ow_ref.shape[0]
    a_ref, at_ref, b_ref, bt_ref = refs[-5:-1]
    ow = ow_ref[...]
    k0, k1 = own_index(masks)
    for s in range(4):
        rows = pl.ds(s * r, r)
        for c in range(4):
            cols = pl.ds(c * r, r)
            a = mw_ref[0, k1 ^ s, k0 ^ c]
            b = dot(ow, mw_ref[1, s, k1 ^ c])
            a_ref[rows, cols] = a
            at_ref[cols, rows] = a.astype(jnp.float32).T.astype(jnp.bfloat16)
            b_ref[rows, cols] = b.astype(jnp.bfloat16)
            bt_ref[cols, rows] = b.T.astype(jnp.bfloat16)


def gate_kernel(*refs):
    pass


def forward_local_kernel(masks, sizes, index, first, *refs):
    image_ref, first_ref, second_ref = refs[:3]
    refs, (tiles, sems, *held) = (refs[:-4], refs[-4:]) if first else (refs[:-2], refs[-2:])
    copies = []
    k0 = own_index(masks)[0]
    for i, (source, target) in enumerate(zip((first_ref, second_ref), held)):
        copies.append(pltpu.make_async_copy(source, target, sems.at[4 + i]))
    for d in range(4):
        copies.append(
            pltpu.make_async_copy(image_ref.at[k0 ^ d, index], tiles.at[d], sems.at[d])
        )
    for copy in copies:
        copy.start()
    if first:
        w0_ref, w1_ref = refs[-3:-1]
        outs = refs[-3 - 4 * len(sizes) : -3]
        levels, inner = held
        r = inner.shape[0]
        for copy in copies[:2]:
            copy.wait()
        copies = copies[2:]
        folded = dot(levels[0].reshape(16 * r, r), inner[...]).astype(jnp.bfloat16)
        w0 = jnp.concatenate(blocks_of(folded.reshape(16, r, r), r), axis=0)
        w1 = jnp.concatenate(blocks_of(levels[1].reshape(16, r, r), r), axis=0)
        w0_ref[...], w1_ref[...] = w0, w1
    else:
        w0, w1 = first_ref[...], second_ref[...]
        outs = refs[-1 - 4 * len(sizes) : -1]
    r, n = tiles.shape[-2:]
    for d in range(4):
        copies[d].wait()
        x = stacked([[tiles[d, 4 * a + c] for a in range(4)] for c in range(4)])
        y = dot(w0, x).astype(jnp.bfloat16)
        x = stacked([[tile(y, e, a, r, n) for e in range(4)] for a in range(4)])
        y = dot(w1, x).astype(jnp.bfloat16)
        start = 0
        for piece, size in enumerate(sizes):
            for h in range(size):
                a, e = divmod(start + h, 4)
                outs[4 * piece + d][h] = tile(y, a, e, r, n)
            start += size


def adjoint_local_kernel(masks, sizes, index, w0t_ref, w1t_ref, *refs):
    ins, out_ref, tiles, sems = refs[: 4 * len(sizes)], refs[-4], refs[-2], refs[-1]
    r, n = tiles.shape[-2:]
    w0t, w1t = w0t_ref[...], w1t_ref[...]
    places = [(piece, h) for piece, size in enumerate(sizes) for h in range(size)]
    k0 = own_index(masks)[0]
    copies = []
    for d in range(4):

        def piece_of(a, e):
            piece, h = places[4 * a + e]
            return ins[4 * piece + d][h]

        x = stacked([[piece_of(a, e) for e in range(4)] for a in range(4)])
        y = dot(w1t, x).astype(jnp.bfloat16)
        x = stacked([[tile(y, a, e, r, n) for a in range(4)] for e in range(4)])
        y = dot(w0t, x).astype(jnp.bfloat16)
        for a in range(4):
            for c in range(4):
                tiles[d, 4 * a + c] = tile(y, c, a, r, n)
        copies.append(
            pltpu.make_async_copy(tiles.at[d], out_ref.at[k0 ^ d, index], sems.at[d])
        )
        copies[-1].start()
    for copy in copies:
        copy.wait()


def merge_kernel(w_ref, *refs):
    ins, outs = refs[:4], refs[-5:-1]
    size, r, n = ins[0].shape
    w = w_ref[...]
    for i in range(0, size, 4):
        x = stacked([[ref[i + j] for j in range(4)] for ref in ins])
        y = dot(w, x).astype(jnp.bfloat16)
        for d in range(4):
            for j in range(4):
                outs[d][i + j] = tile(y, d, j, r, n)


def residual_kernel(start, b_ref, bt_ref, phases_ref, observed_ref, *refs):
    ins, outs, (angles, data, sems) = refs[:4], refs[-8:-4], refs[-3:]
    size, r, n = ins[0].shape
    copies = []
    for i in range(size // 4):
        here, there = pl.ds(4 * i, 4), pl.ds(start + 4 * i, 4)
        copies.append(
            (
                pltpu.make_async_copy(phases_ref.at[:, there], angles.at[:, here], sems.at[0, i]),
                pltpu.make_async_copy(observed_ref.at[:, there], data.at[:, here], sems.at[1, i]),
            )
        )
        for copy in copies[-1]:
            copy.start()
    for i in range(size // 4):
        x = stacked([[ref[4 * i + j] for j in range(4)] for ref in ins])
        predicted = dot(b_ref[...], x)
        for copy in copies[i]:
            copy.wait()
        weighted = []
        for s in range(4):
            row = []
            for j in range(4):
                wave = cas(angles[s, 4 * i + j])
                residual = wave * tile(predicted, s, j, r, n)
                residual = residual - data[s, 4 * i + j].astype(jnp.float32)
                residual = residual.astype(jnp.bfloat16).astype(jnp.float32)
                row.append((wave * residual).astype(jnp.bfloat16))
            weighted.append(row)
        y = dot(bt_ref[...], stacked(weighted)).astype(jnp.bfloat16)
        for d in range(4):
            for j in range(4):
                outs[d][4 * i + j] = tile(y, d, j, r, n)


VMEM = pl.BlockSpec(memory_space=pltpu.VMEM)
ANY = pl.BlockSpec(memory_space=pl.ANY)
HBM = pl.BlockSpec(memory_space=pltpu.HBM)


KERNEL_COST = pl.CostEstimate(flops=0, bytes_accessed=0, transcendentals=0)
GATE_COST = pl.CostEstimate(flops=10**9, bytes_accessed=1, transcendentals=0)


class Chain:
    def __init__(self, masks):
        self.token = None
        self.done = []
        count_x, count_y = lax.axis_size("qx"), lax.axis_size("qy")
        self.pairs = []
        for mask_x, mask_y in masks:
            along_y = [(s, s ^ mask_y) for s in range(count_y)]
            along_x = [(s, s ^ mask_x) for s in range(count_x)]
            both = [
                (x * count_y + y, (x ^ mask_x) * count_y + (y ^ mask_y))
                for x in range(count_x)
                for y in range(count_y)
            ]
            self.pairs.append((None, ("qy", along_y), ("qx", along_x), (("qx", "qy"), both)))

    def kernel(
        self, body, operands, specs, out_shapes, out_specs, aliases=None, gate=False, **options
    ):
        extra = [x for x in self.done if not any(x is y for y in operands)]
        self.done = []
        aliases = dict(aliases or {})
        token = [] if self.token is None else [self.token]
        if token:
            aliases[len(operands)] = len(out_shapes)
        outs = pl.pallas_call(
            body,
            out_shape=[*out_shapes, TOKEN],
            in_specs=[*specs, *[ANY] * (len(token) + len(extra))],
            out_specs=[*out_specs, ANY],
            input_output_aliases=aliases,
            compiler_params=pltpu.CompilerParams(vmem_limit_bytes=2**20 if gate else VMEM_GRANT),
            cost_estimate=GATE_COST if gate else KERNEL_COST,
            **options,
        )(*operands, *token, *extra)
        self.token = outs[-1]
        return outs[:-1]

    def send(self, block, level, d):
        shape = jax.ShapeDtypeStruct(block.shape, block.dtype)
        (block,) = self.kernel(gate_kernel, [block], [ANY], [shape], [ANY], {0: 0}, True)
        axis, pairs = self.pairs[level][d]
        return lax.ppermute(block, axis, pairs)


def local(image_tiles, observed, phases, interpolate, local_weights, merge_weights, output_weight):
    groups, r, n = image_tiles.shape[2:]
    depth = merge_weights.shape[2]
    chunks = len(PIECES)
    quarter = groups // 4
    chunk = quarter // chunks
    bf16 = jnp.bfloat16
    box = r * n * 2

    masks = []
    for level in range(depth):
        bit_x = level_bit(lax.axis_size("qx"), level, depth)
        bit_y = level_bit(lax.axis_size("qy"), level, depth)
        masks.append((2**bit_x, 2**bit_y))
    square = jax.ShapeDtypeStruct((4 * r, 4 * r), bf16)
    chain = Chain(masks)

    def pinned(x, shape):
        return pltpu.with_memory_space_constraint(x.reshape(shape), pltpu.HBM)

    image = pinned(image_tiles, (4, chunks, chunk, r, n))
    phase4 = pinned(phases, (4, quarter, r, n))
    observed4 = pinned(observed, (4, quarter, r, n))
    levels = pinned(local_weights, local_weights.shape[2:])
    inner = pinned(interpolate, interpolate.shape)

    def shapes(size):
        return [jax.ShapeDtypeStruct((size, r, n), bf16)] * 4

    def forward_local(index):
        sizes = PIECES[index]
        first = not prepared
        weights = [levels, inner] if first else list(prepared["local"])
        scratch = [pltpu.VMEM((4, chunk, r, n), bf16), pltpu.SemaphoreType.DMA((6,))]
        if first:
            scratch += [pltpu.VMEM(levels.shape, bf16), pltpu.VMEM((r, r), bf16)]
        outs_count = 4 * len(sizes) + 2 * first
        with jax.named_scope(f"local_forward_{index}"):
            outs = chain.kernel(
                functools.partial(forward_local_kernel, masks, sizes, index, first),
                [image, *weights],
                [HBM] + [HBM if first else VMEM] * 2,
                sum([shapes(size) for size in sizes], []) + [square] * (2 * first),
                [VMEM] * outs_count,
                scratch_shapes=scratch,
            )
        if first:
            prepared["local"] = outs[-2:]
        for piece in range(len(sizes)):
            ready["X0", first_piece[index] + piece] = outs[4 * piece : 4 * piece + 4]

    def prepare_merges():
        with jax.named_scope("prep_merge"):
            prepared["merge"] = chain.kernel(
                functools.partial(prep_merge_kernel, masks),
                [merge_weights[0, 0], output_weight],
                [VMEM, VMEM],
                [square] * 4,
                [VMEM] * 4,
            )

    def prepare_adjoint():
        with jax.named_scope("prep_adjoint"):
            prepared["adjoint"] = chain.kernel(
                prep_adjoint_kernel,
                [local_weights[0, 0], interpolate],
                [VMEM, VMEM],
                [square] * 2,
                [VMEM] * 2,
            )

    def merge(weight, blocks):
        size = blocks[0].shape[0]
        return chain.kernel(
            merge_kernel,
            [weight, *blocks],
            [VMEM] * 5,
            shapes(size),
            [VMEM] * 4,
        )

    def through_data(blocks, start):
        size = blocks[0].shape[0]
        return chain.kernel(
            functools.partial(residual_kernel, start),
            [*prepared["merge"][2:], phase4, observed4, *blocks],
            [VMEM, VMEM, HBM, HBM] + [VMEM] * 4,
            shapes(size),
            [VMEM] * 4,
            scratch_shapes=[
                pltpu.VMEM((4, size, r, n), jnp.float32),
                pltpu.VMEM((4, size, r, n), bf16),
                pltpu.SemaphoreType.DMA((2, size // 4)),
            ],
        )

    def adjoint_local(index):
        sizes = PIECES[index]
        blocks = sum([state["Y0", first_piece[index] + i] for i in range(len(sizes))], [])
        operands = [*prepared["adjoint"], *blocks]
        specs = [VMEM] * len(operands)
        aliases = {}
        if "gradient" in prepared:
            aliases = {len(operands): 0}
            operands.append(prepared["gradient"])
            specs.append(HBM)
        with jax.named_scope(f"local_adjoint_{index}"):
            (prepared["gradient"],) = chain.kernel(
                functools.partial(adjoint_local_kernel, masks, sizes, index),
                operands,
                specs,
                [jax.ShapeDtypeStruct((4, chunks, chunk, r, n), bf16)],
                [HBM],
                aliases,
                scratch_shapes=[
                    pltpu.VMEM((4, chunk, r, n), bf16),
                    pltpu.SemaphoreType.DMA((4,)),
                ],
            )

    all_sizes = sum(PIECES, ())
    starts = [sum(all_sizes[:i]) for i in range(len(all_sizes))]
    first_piece = [sum(len(p) for p in PIECES[:i]) for i in range(chunks)]
    prepared, ready, state = {}, {}, {}

    for action in ACTIONS:
        mark, name, number = action[0], action[-4:-2], int(action[-2])
        if mark == ".":
            with jax.named_scope(f"{name}_{number}"):
                if name == "K1":
                    forward_local(number)
                elif name == "PM":
                    prepare_merges()
                elif name == "PA":
                    prepare_adjoint()
                elif name == "X1":
                    ready["X1", number] = merge(prepared["merge"][0], state["X0", number])
                elif name == "Y1":
                    ready["Y1", number] = through_data(state["X1", number], starts[number])
                elif name == "Y0":
                    ready["Y0", number] = merge(prepared["merge"][1], state["Y1", number])
                else:
                    adjoint_local(number)
            continue
        d = {"z": 1, "x": 2, "d": 3}[action[-1]]
        if mark == "+":
            blocks = ready[name, number]
            got = state.setdefault((name, number), [blocks[0], None, None, None])
            with jax.named_scope(f"{name}_{number}"):
                got[d] = chain.send(blocks[d], 1 if name in ("X1", "Y1") else 0, d)
        else:
            chain.done.append(state[name, number][d])
    return prepared["gradient"].reshape(1, 1, groups, r, n)


def solution(mesh):
    split = P("qx", "qy", None, None, None)
    weights = P("qx", "qy", None, None, None, None, None)
    return jax.shard_map(
        local,
        mesh=mesh,
        in_specs=(split, split, split, P(), weights, weights, P()),
        out_specs=split,
        check_vma=False,
    )
```

```python
import functools

import jax
import jax.numpy as jnp
import numpy as np
from jax import lax
from jax.experimental import pallas as pl
from jax.experimental.pallas import tpu as pltpu
from jax.sharding import PartitionSpec as P

X_PIECES = ((16,), (16,), (16,), (16,))
Y_PIECES = ((16,), (16,), (16,), (8, 8))
ACTIONS = (
    ".K10_", "+X00z", ".K13_", "+X03x", "+X00d", ".K11_", "+X01x", "+X00x", ".PM0_", ".K12_",
    "-X00z", "+X01d", "-X03x", "+X01z", "-X00d", "-X01x", "-X00x", ".X10_", "+X10d", "+X10x",
    "+X10z", "-X01d", "-X01z", ".X11_", "+X11x", "+X02d", "-X10d", "+X11z", "-X10x", "+X02x",
    ".PA0_", "-X10z", "+X02z", "-X11x", "+X11d", ".Y10_", "-X02d", "+Y10z", "-X11z", "+X03z",
    "-X02x", "+X03d", "-X02z", ".X12_", "+X12d", "-X11d", "+Y10x", ".Y11_", "-Y10z", "+X12z",
    "-X03z", "+Y11d", "-X03d", "+Y10d", "-X12d", "+Y11x", ".X13_", "-Y10x", "+X13z", "-X12z",
    "+X12x", "-Y11d", "+Y11z", "-Y10d", "+X13x", ".Y00_", "-Y11x", "+Y00d", "-X13z", "+X13d",
    "-X12x", "+Y00z", ".Y12_", "-Y11z", "+Y12x", "-X13x", "+Y12z", ".Y01_", "-Y00d", "+Y01d",
    "-X13d", ".Y13_", "+Y13x", "-Y00z", "+Y12d", "-Y12x", "+Y01z", ".Y14_", "-Y12z", "+Y01x",
    "-Y01d", "+Y14z", "-Y13x", "+Y14x", "-Y12d", ".Y02_", "+Y02d", "-Y01z", "+Y13z", "-Y01x",
    "+Y14d", "-Y14z", "+Y02z", "-Y14x", "+Y13d", ".K51_", "-Y02d", "-Y13z", "-Y14d", ".Y04_",
    "+Y04z", "+Y00x", "+Y02x", "-Y02z", "+Y04d", "-Y13d", ".Y03_", "+Y03d", "-Y04z", "+Y04x",
    "-Y00x", "+Y03z", "-Y02x", "+Y03x", ".K50_", ".K52_", "-Y04d", "-Y03d", "-Y04x", "-Y03z",
    "-Y03x", ".K53_",
)
VMEM_GRANT = 16 * 2**20
TOKEN = jax.ShapeDtypeStruct((8, 128), jnp.float32)
QUARTER_PI, HALF_PI = float(np.pi / 4), float(np.pi / 2)
SINE = (
    -1.4142135381698608,
    0.23570221662521362,
    -0.011785031296312809,
    0.00028053473215550184,
    -3.875064521707827e-06,
    3.182795182965492e-08,
)


def level_bit(axis_count, level_index, depth):
    total_bits = axis_count.bit_length() - 1
    return level_index * (total_bits - 1) // max(depth - 1, 1)


def dot(a, b):
    return jnp.dot(a, b, preferred_element_type=jnp.float32)


def cas(angle):
    rest = jnp.abs(angle - QUARTER_PI) - HALF_PI
    square = rest * rest
    poly = jnp.float32(SINE[-1])
    for c in SINE[-2::-1]:
        poly = poly * square + jnp.float32(c)
    return poly * rest


def stacked(columns):
    return jnp.concatenate([jnp.concatenate(row, axis=1) for row in columns], axis=0)


def tile(y, i, j, r, n):
    return y[i * r : (i + 1) * r, j * n : (j + 1) * n]


def own_index(masks):
    x, y = lax.axis_index("qx"), lax.axis_index("qy")
    return [
        2 * jnp.where(x & mask_x != 0, 1, 0) + jnp.where(y & mask_y != 0, 1, 0)
        for mask_x, mask_y in masks
    ]


def blocks_of(stack, r):
    return [
        jnp.concatenate([stack[4 * k + c] for c in range(4)], axis=1) for k in range(4)
    ]


def prep_adjoint_kernel(lw_ref, ip_ref, *refs):
    r = ip_ref.shape[0]
    w0t_ref, w1t_ref = refs[-3:-1]
    ip = ip_ref[...]
    for k in range(4):
        cols = pl.ds(k * r, r)
        for c in range(4):
            rows = pl.ds(c * r, r)
            w0t_ref[rows, cols] = dot(lw_ref[0, k, c], ip).T.astype(jnp.bfloat16)
            w1t_ref[rows, cols] = lw_ref[1, k, c].astype(jnp.float32).T.astype(jnp.bfloat16)


def prep_merge_kernel(masks, mw_ref, ow_ref, *refs):
    r = ow_ref.shape[0]
    a_ref, at_ref, b_ref, bt_ref = refs[-5:-1]
    ow = ow_ref[...]
    k0, k1 = own_index(masks)
    for s in range(4):
        rows = pl.ds(s * r, r)
        for c in range(4):
            cols = pl.ds(c * r, r)
            a = mw_ref[0, k1 ^ s, k0 ^ c]
            b = dot(ow, mw_ref[1, s, k1 ^ c])
            a_ref[rows, cols] = a
            at_ref[cols, rows] = a.astype(jnp.float32).T.astype(jnp.bfloat16)
            b_ref[rows, cols] = b.astype(jnp.bfloat16)
            bt_ref[cols, rows] = b.T.astype(jnp.bfloat16)


def gate_kernel(*refs):
    pass


def forward_local_kernel(masks, sizes, index, first, *refs):
    image_ref, first_ref, second_ref = refs[:3]
    refs, (tiles, sems, *held) = (refs[:-4], refs[-4:]) if first else (refs[:-2], refs[-2:])
    copies = []
    k0 = own_index(masks)[0]
    for i, (source, target) in enumerate(zip((first_ref, second_ref), held)):
        copies.append(pltpu.make_async_copy(source, target, sems.at[4 + i]))
    for d in range(4):
        copies.append(
            pltpu.make_async_copy(image_ref.at[k0 ^ d, index], tiles.at[d], sems.at[d])
        )
    for copy in copies:
        copy.start()
    if first:
        w0_ref, w1_ref = refs[-3:-1]
        outs = refs[-3 - 4 * len(sizes) : -3]
        levels, inner = held
        r = inner.shape[0]
        for copy in copies[:2]:
            copy.wait()
        copies = copies[2:]
        folded = dot(levels[0].reshape(16 * r, r), inner[...]).astype(jnp.bfloat16)
        w0 = jnp.concatenate(blocks_of(folded.reshape(16, r, r), r), axis=0)
        w1 = jnp.concatenate(blocks_of(levels[1].reshape(16, r, r), r), axis=0)
        w0_ref[...], w1_ref[...] = w0, w1
    else:
        w0, w1 = first_ref[...], second_ref[...]
        outs = refs[-1 - 4 * len(sizes) : -1]
    r, n = tiles.shape[-2:]
    for d in range(4):
        copies[d].wait()
        x = stacked([[tiles[d, 4 * a + c] for a in range(4)] for c in range(4)])
        y = dot(w0, x).astype(jnp.bfloat16)
        x = stacked([[tile(y, e, a, r, n) for e in range(4)] for a in range(4)])
        y = dot(w1, x).astype(jnp.bfloat16)
        start = 0
        for piece, size in enumerate(sizes):
            for h in range(size):
                a, e = divmod(start + h, 4)
                outs[4 * piece + d][h] = tile(y, a, e, r, n)
            start += size


def adjoint_local_kernel(masks, sizes, index, w0t_ref, w1t_ref, *refs):
    ins, out_ref, tiles, sems = refs[: 4 * len(sizes)], refs[-4], refs[-2], refs[-1]
    r, n = tiles.shape[-2:]
    w0t, w1t = w0t_ref[...], w1t_ref[...]
    places = [(piece, h) for piece, size in enumerate(sizes) for h in range(size)]
    k0 = own_index(masks)[0]
    copies = []
    for d in range(4):

        def piece_of(a, e):
            piece, h = places[4 * a + e]
            return ins[4 * piece + d][h]

        x = stacked([[piece_of(a, e) for e in range(4)] for a in range(4)])
        y = dot(w1t, x).astype(jnp.bfloat16)
        x = stacked([[tile(y, a, e, r, n) for a in range(4)] for e in range(4)])
        y = dot(w0t, x).astype(jnp.bfloat16)
        for a in range(4):
            for c in range(4):
                tiles[d, 4 * a + c] = tile(y, c, a, r, n)
        copies.append(
            pltpu.make_async_copy(tiles.at[d], out_ref.at[k0 ^ d, index], sems.at[d])
        )
        copies[-1].start()
    for copy in copies:
        copy.wait()


def merge_kernel(w_ref, *refs):
    ins, outs = refs[:4], refs[-5:-1]
    size, r, n = ins[0].shape
    w = w_ref[...]
    for i in range(0, size, 4):
        x = stacked([[ref[i + j] for j in range(4)] for ref in ins])
        y = dot(w, x).astype(jnp.bfloat16)
        for d in range(4):
            for j in range(4):
                outs[d][i + j] = tile(y, d, j, r, n)


def residual_kernel(start, sources, b_ref, bt_ref, phases_ref, observed_ref, *refs):
    outs, (angles, data, sems) = refs[-8:-4], refs[-3:]
    r, n = outs[0].shape[1:]
    copies = []
    for i in range(len(sources)):
        here, there = pl.ds(4 * i, 4), pl.ds(start + 4 * i, 4)
        copies.append(
            (
                pltpu.make_async_copy(phases_ref.at[:, there], angles.at[:, here], sems.at[0, i]),
                pltpu.make_async_copy(observed_ref.at[:, there], data.at[:, here], sems.at[1, i]),
            )
        )
        for copy in copies[-1]:
            copy.start()
    for i, (source, first) in enumerate(sources):
        ins = refs[4 * source : 4 * source + 4]
        x = stacked([[ref[first + j] for j in range(4)] for ref in ins])
        predicted = dot(b_ref[...], x)
        for copy in copies[i]:
            copy.wait()
        weighted = []
        for s in range(4):
            row = []
            for j in range(4):
                wave = cas(angles[s, 4 * i + j])
                residual = wave * tile(predicted, s, j, r, n)
                residual = residual - data[s, 4 * i + j].astype(jnp.float32)
                residual = residual.astype(jnp.bfloat16).astype(jnp.float32)
                row.append((wave * residual).astype(jnp.bfloat16))
            weighted.append(row)
        y = dot(bt_ref[...], stacked(weighted)).astype(jnp.bfloat16)
        for d in range(4):
            for j in range(4):
                outs[d][4 * i + j] = tile(y, d, j, r, n)


VMEM = pl.BlockSpec(memory_space=pltpu.VMEM)
ANY = pl.BlockSpec(memory_space=pl.ANY)
HBM = pl.BlockSpec(memory_space=pltpu.HBM)


KERNEL_COST = pl.CostEstimate(flops=0, bytes_accessed=0, transcendentals=0)
GATE_COST = pl.CostEstimate(flops=1000000000, bytes_accessed=1, transcendentals=0)


class Chain:
    def __init__(self, masks):
        self.token = None
        self.done = []
        count_x, count_y = lax.axis_size("qx"), lax.axis_size("qy")
        self.pairs = []
        for mask_x, mask_y in masks:
            along_y = [(s, s ^ mask_y) for s in range(count_y)]
            along_x = [(s, s ^ mask_x) for s in range(count_x)]
            both = [
                (x * count_y + y, (x ^ mask_x) * count_y + (y ^ mask_y))
                for x in range(count_x)
                for y in range(count_y)
            ]
            self.pairs.append((None, ("qy", along_y), ("qx", along_x), (("qx", "qy"), both)))

    def kernel(
        self, body, operands, specs, out_shapes, out_specs, aliases=None, gate=False, **options
    ):
        extra = [x for x in self.done if not any(x is y for y in operands)]
        self.done = []
        aliases = dict(aliases or {})
        token = [] if self.token is None else [self.token]
        if token:
            aliases[len(operands)] = len(out_shapes)
        outs = pl.pallas_call(
            body,
            out_shape=[*out_shapes, TOKEN],
            in_specs=[*specs, *[ANY] * (len(token) + len(extra))],
            out_specs=[*out_specs, ANY],
            input_output_aliases=aliases,
            compiler_params=pltpu.CompilerParams(vmem_limit_bytes=2**20 if gate else VMEM_GRANT),
            cost_estimate=GATE_COST if gate else KERNEL_COST,
            **options,
        )(*operands, *token, *extra)
        self.token = outs[-1]
        return outs[:-1]

    def send(self, block, level, d):
        shape = jax.ShapeDtypeStruct(block.shape, block.dtype)
        with jax.named_scope("gate_mark"):
            (block,) = self.kernel(gate_kernel, [block], [ANY], [shape], [ANY], {0: 0}, True)
        axis, pairs = self.pairs[level][d]
        return lax.ppermute(block, axis, pairs)


def local(image_tiles, observed, phases, interpolate, local_weights, merge_weights, output_weight):
    groups, r, n = image_tiles.shape[2:]
    depth = merge_weights.shape[2]
    chunks = len(X_PIECES)
    quarter = groups // 4
    chunk = quarter // chunks
    bf16 = jnp.bfloat16

    masks = []
    for level in range(depth):
        bit_x = level_bit(lax.axis_size("qx"), level, depth)
        bit_y = level_bit(lax.axis_size("qy"), level, depth)
        masks.append((2**bit_x, 2**bit_y))
    square = jax.ShapeDtypeStruct((4 * r, 4 * r), bf16)
    chain = Chain(masks)

    def pinned(x, shape):
        return pltpu.with_memory_space_constraint(x.reshape(shape), pltpu.HBM)

    image = pinned(image_tiles, (4, chunks, chunk, r, n))
    phase4 = pinned(phases, (4, quarter, r, n))
    observed4 = pinned(observed, (4, quarter, r, n))
    levels = pinned(local_weights, local_weights.shape[2:])
    inner = pinned(interpolate, interpolate.shape)

    def shapes(size):
        return [jax.ShapeDtypeStruct((size, r, n), bf16)] * 4

    def forward_local(index):
        sizes = X_PIECES[index]
        first = not prepared
        weights = [levels, inner] if first else list(prepared["local"])
        scratch = [pltpu.VMEM((4, chunk, r, n), bf16), pltpu.SemaphoreType.DMA((6,))]
        if first:
            scratch += [pltpu.VMEM(levels.shape, bf16), pltpu.VMEM((r, r), bf16)]
        outs_count = 4 * len(sizes) + 2 * first
        with jax.named_scope(f"local_forward_{index}"):
            outs = chain.kernel(
                functools.partial(forward_local_kernel, masks, sizes, index, first),
                [image, *weights],
                [HBM] + [HBM if first else VMEM] * 2,
                sum([shapes(size) for size in sizes], []) + [square] * (2 * first),
                [VMEM] * outs_count,
                scratch_shapes=scratch,
            )
        if first:
            prepared["local"] = outs[-2:]
        for piece in range(len(sizes)):
            ready["X0", x_first[index] + piece] = outs[4 * piece : 4 * piece + 4]

    def prepare_merges():
        with jax.named_scope("prep_merge"):
            prepared["merge"] = chain.kernel(
                functools.partial(prep_merge_kernel, masks),
                [merge_weights[0, 0], output_weight],
                [VMEM, VMEM],
                [square] * 4,
                [VMEM] * 4,
            )

    def prepare_adjoint():
        with jax.named_scope("prep_adjoint"):
            prepared["adjoint"] = chain.kernel(
                prep_adjoint_kernel,
                [local_weights[0, 0], interpolate],
                [VMEM, VMEM],
                [square] * 2,
                [VMEM] * 2,
            )

    def merge(weight, blocks):
        size = blocks[0].shape[0]
        return chain.kernel(
            merge_kernel,
            [weight, *blocks],
            [VMEM] * 5,
            shapes(size),
            [VMEM] * 4,
        )

    def through_data(number):
        start, size = y_starts[number], y_sizes[number]
        inside = [
            p for p, (a, m) in enumerate(zip(x_starts, x_sizes)) if a < start + size and start < a + m
        ]
        sources = []
        for box in range(start, start + size, 4):
            k = [i for i, p in enumerate(inside) if 0 <= box - x_starts[p] < x_sizes[p]][0]
            sources.append((k, box - x_starts[inside[k]]))
        blocks = sum([state["X1", p] for p in inside], [])
        return chain.kernel(
            functools.partial(residual_kernel, start, sources),
            [*prepared["merge"][2:], phase4, observed4, *blocks],
            [VMEM, VMEM, HBM, HBM] + [VMEM] * len(blocks),
            shapes(size),
            [VMEM] * 4,
            scratch_shapes=[
                pltpu.VMEM((4, size, r, n), jnp.float32),
                pltpu.VMEM((4, size, r, n), bf16),
                pltpu.SemaphoreType.DMA((2, size // 4)),
            ],
        )

    def adjoint_local(index):
        sizes = Y_PIECES[index]
        blocks = sum([state["Y0", y_first[index] + i] for i in range(len(sizes))], [])
        operands = [*prepared["adjoint"], *blocks]
        specs = [VMEM] * len(operands)
        aliases = {}
        if "gradient" in prepared:
            aliases = {len(operands): 0}
            operands.append(prepared["gradient"])
            specs.append(HBM)
        with jax.named_scope(f"local_adjoint_{index}"):
            (prepared["gradient"],) = chain.kernel(
                functools.partial(adjoint_local_kernel, masks, sizes, index),
                operands,
                specs,
                [jax.ShapeDtypeStruct((4, chunks, chunk, r, n), bf16)],
                [HBM],
                aliases,
                scratch_shapes=[
                    pltpu.VMEM((4, chunk, r, n), bf16),
                    pltpu.SemaphoreType.DMA((4,)),
                ],
            )

    x_sizes, y_sizes = sum(X_PIECES, ()), sum(Y_PIECES, ())
    x_starts = [sum(x_sizes[:i]) for i in range(len(x_sizes))]
    y_starts = [sum(y_sizes[:i]) for i in range(len(y_sizes))]
    x_first = [sum(len(p) for p in X_PIECES[:i]) for i in range(chunks)]
    y_first = [sum(len(p) for p in Y_PIECES[:i]) for i in range(chunks)]
    prepared, ready, state = {}, {}, {}

    for action in ACTIONS:
        mark, name, number = action[0], action[-4:-2], int(action[-2])
        if mark == ".":
            with jax.named_scope(f"{name}_{number}"):
                if name == "K1":
                    forward_local(number)
                elif name == "PM":
                    prepare_merges()
                elif name == "PA":
                    prepare_adjoint()
                elif name == "X1":
                    ready["X1", number] = merge(prepared["merge"][0], state["X0", number])
                elif name == "Y1":
                    ready["Y1", number] = through_data(number)
                elif name == "Y0":
                    ready["Y0", number] = merge(prepared["merge"][1], state["Y1", number])
                else:
                    adjoint_local(number)
            continue
        d = {"z": 1, "x": 2, "d": 3}[action[-1]]
        if mark == "+":
            blocks = ready[name, number]
            got = state.setdefault((name, number), [blocks[0], None, None, None])
            with jax.named_scope(f"{name}_{number}"):
                got[d] = chain.send(blocks[d], 1 if name in ("X1", "Y1") else 0, d)
        else:
            chain.done.append(state[name, number][d])
    return prepared["gradient"].reshape(1, 1, groups, r, n)


def solution(mesh):
    split = P("qx", "qy", None, None, None)
    weights = P("qx", "qy", None, None, None, None, None)
    return jax.shard_map(
        local,
        mesh=mesh,
        in_specs=(split, split, split, P(), weights, weights, P()),
        out_specs=split,
        check_vma=False,
    )
```

```python
import functools

import jax
import jax.numpy as jnp
import numpy as np
from jax import lax
from jax.experimental import pallas as pl
from jax.experimental.pallas import tpu as pltpu
from jax.sharding import PartitionSpec as P

X_PIECES = ((16,), (16,), (16,), (16,))
Y_PIECES = ((16,), (16,), (16,), (8, 8))
ACTIONS = (
    ".K10_", "+X00z", ".K13_", "+X03x", "+X00d", ".K11_", "+X01x", "+X00x", ".PM0_", ".K12_",
    "-X00z", "+X01d", "-X03x", "+X01z", "-X00d", "-X01x", "-X00x", ".X10_", "+X10d", "+X10x",
    "+X10z", "-X01d", "-X01z", ".X11_", "+X11x", "+X02d", "-X10d", "+X11z", "-X10x", "+X02x",
    ".PA0_", "-X10z", "+X02z", "-X11x", "+X11d", ".Y10_", "-X02d", "+Y10z", "-X11z", "+X03z",
    "-X02x", "+X03d", "-X02z", ".X12_", "+X12d", "-X11d", "+Y10x", ".Y11_", "-Y10z", "+X12z",
    "-X03z", "+Y11d", "-X03d", "+Y10d", "-X12d", "+Y11x", ".X13_", "-Y10x", "+X13z", "-X12z",
    "+X12x", "-Y11d", "+Y11z", "-Y10d", "+X13x", ".Y00_", "-Y11x", "+Y00d", "-X13z", "+X13d",
    "-X12x", "+Y00z", ".Y12_", "-Y11z", "+Y12x", "-X13x", "+Y12z", ".Y01_", "-Y00d", "+Y01d",
    "-X13d", ".Y13_", "+Y13x", "-Y00z", "+Y12d", "-Y12x", "+Y01z", ".Y14_", "-Y12z", "+Y01x",
    "-Y01d", "+Y14z", "-Y13x", "+Y14x", "-Y12d", ".Y02_", "+Y02d", "-Y01z", "+Y13z", "-Y01x",
    "+Y14d", "-Y14z", "+Y02z", "-Y14x", "+Y13d", ".K51_", "-Y02d", "-Y13z", "-Y14d", ".Y04_",
    "+Y04z", "+Y00x", "+Y02x", "-Y02z", "+Y04d", "-Y13d", ".Y03_", "+Y03d", "-Y04z", "+Y04x",
    "-Y00x", "+Y03z", "-Y02x", "+Y03x", ".K50_", ".K52_", "-Y04d", "-Y03d", "-Y04x", "-Y03z",
    "-Y03x", ".K53_",
)
VMEM_GRANT = 16 * 2**20
TOKEN = jax.ShapeDtypeStruct((8, 128), jnp.float32)
QUARTER_PI, HALF_PI = float(np.pi / 4), float(np.pi / 2)
SINE = (
    -1.4142135381698608,
    0.23570221662521362,
    -0.011785031296312809,
    0.00028053473215550184,
    -3.875064521707827e-06,
    3.182795182965492e-08,
)


def level_bit(axis_count, level_index, depth):
    total_bits = axis_count.bit_length() - 1
    return level_index * (total_bits - 1) // max(depth - 1, 1)


def dot(a, b):
    return jnp.dot(a, b, preferred_element_type=jnp.float32)


def cas(angle):
    rest = jnp.abs(angle - QUARTER_PI) - HALF_PI
    square = rest * rest
    poly = jnp.float32(SINE[-1])
    for c in SINE[-2::-1]:
        poly = poly * square + jnp.float32(c)
    return poly * rest


def stacked(columns):
    return jnp.concatenate([jnp.concatenate(row, axis=1) for row in columns], axis=0)


def tile(y, i, j, r, n):
    return y[i * r : (i + 1) * r, j * n : (j + 1) * n]


def own_index(masks):
    x, y = lax.axis_index("qx"), lax.axis_index("qy")
    return [
        2 * jnp.where(x & mask_x != 0, 1, 0) + jnp.where(y & mask_y != 0, 1, 0)
        for mask_x, mask_y in masks
    ]


def blocks_of(stack, r):
    return [
        jnp.concatenate([stack[4 * k + c] for c in range(4)], axis=1) for k in range(4)
    ]


def prep_adjoint_kernel(lw_ref, ip_ref, *refs):
    r = ip_ref.shape[0]
    w0t_ref, w1t_ref = refs[-3:-1]
    ip = ip_ref[...]
    for k in range(4):
        cols = pl.ds(k * r, r)
        for c in range(4):
            rows = pl.ds(c * r, r)
            w0t_ref[rows, cols] = dot(lw_ref[0, k, c], ip).T.astype(jnp.bfloat16)
            w1t_ref[rows, cols] = lw_ref[1, k, c].astype(jnp.float32).T.astype(jnp.bfloat16)


def prep_merge_kernel(masks, mw_ref, ow_ref, *refs):
    r = ow_ref.shape[0]
    a_ref, at_ref, b_ref, bt_ref = refs[-5:-1]
    ow = ow_ref[...]
    k0, k1 = own_index(masks)
    for s in range(4):
        rows = pl.ds(s * r, r)
        for c in range(4):
            cols = pl.ds(c * r, r)
            a = mw_ref[0, k1 ^ s, k0 ^ c]
            b = dot(ow, mw_ref[1, s, k1 ^ c])
            a_ref[rows, cols] = a
            at_ref[cols, rows] = a.astype(jnp.float32).T.astype(jnp.bfloat16)
            b_ref[rows, cols] = b.astype(jnp.bfloat16)
            bt_ref[cols, rows] = b.T.astype(jnp.bfloat16)


def gate_kernel(*refs):
    pass


def forward_local_kernel(masks, sizes, index, first, *refs):
    image_ref, first_ref, second_ref = refs[:3]
    refs, (tiles, sems, *held) = (refs[:-4], refs[-4:]) if first else (refs[:-2], refs[-2:])
    copies = []
    k0 = own_index(masks)[0]
    if first:
        for i, (source, target) in enumerate(
            ((first_ref.at[0], held[0].at[0]), (second_ref, held[1]), (first_ref.at[1], held[0].at[1]))
        ):
            copies.append(pltpu.make_async_copy(source, target, sems.at[4 + i]))
    for d in range(4):
        copies.append(
            pltpu.make_async_copy(image_ref.at[k0 ^ d, index], tiles.at[d], sems.at[d])
        )
    for copy in copies:
        copy.start()
    if first:
        w0_ref, w1_ref = refs[-3:-1]
        outs = refs[-3 - 4 * len(sizes) : -3]
        levels, inner = held
        r = inner.shape[0]
        for copy in copies[:2]:
            copy.wait()
        late, copies = copies[2], copies[3:]
        folded = dot(levels[0].reshape(16 * r, r), inner[...]).astype(jnp.bfloat16)
        w0 = jnp.concatenate(blocks_of(folded.reshape(16, r, r), r), axis=0)
        w0_ref[...] = w0
    else:
        w0, w1 = first_ref[...], second_ref[...]
        outs = refs[-1 - 4 * len(sizes) : -1]
    r, n = tiles.shape[-2:]
    for d in range(4):
        copies[d].wait()
        x = stacked([[tiles[d, 4 * a + c] for a in range(4)] for c in range(4)])
        y = dot(w0, x).astype(jnp.bfloat16)
        if first and d == 0:
            late.wait()
            w1 = jnp.concatenate(blocks_of(levels[1].reshape(16, r, r), r), axis=0)
            w1_ref[...] = w1
        x = stacked([[tile(y, e, a, r, n) for e in range(4)] for a in range(4)])
        y = dot(w1, x).astype(jnp.bfloat16)
        start = 0
        for piece, size in enumerate(sizes):
            for h in range(size):
                a, e = divmod(start + h, 4)
                outs[4 * piece + d][h] = tile(y, a, e, r, n)
            start += size


def adjoint_local_kernel(masks, sizes, index, w0t_ref, w1t_ref, *refs):
    ins, out_ref, tiles, sems = refs[: 4 * len(sizes)], refs[-4], refs[-2], refs[-1]
    r, n = tiles.shape[-2:]
    w0t, w1t = w0t_ref[...], w1t_ref[...]
    places = [(piece, h) for piece, size in enumerate(sizes) for h in range(size)]
    k0 = own_index(masks)[0]
    copies = []
    for d in range(4):

        def piece_of(a, e):
            piece, h = places[4 * a + e]
            return ins[4 * piece + d][h]

        x = stacked([[piece_of(a, e) for e in range(4)] for a in range(4)])
        y = dot(w1t, x).astype(jnp.bfloat16)
        x = stacked([[tile(y, a, e, r, n) for a in range(4)] for e in range(4)])
        y = dot(w0t, x).astype(jnp.bfloat16)
        for a in range(4):
            for c in range(4):
                tiles[d, 4 * a + c] = tile(y, c, a, r, n)
        copies.append(
            pltpu.make_async_copy(tiles.at[d], out_ref.at[k0 ^ d, index], sems.at[d])
        )
        copies[-1].start()
    for copy in copies:
        copy.wait()


def merge_kernel(w_ref, *refs):
    ins, outs = refs[:4], refs[-5:-1]
    size, r, n = ins[0].shape
    w = w_ref[...]
    for i in range(0, size, 4):
        x = stacked([[ref[i + j] for j in range(4)] for ref in ins])
        y = dot(w, x).astype(jnp.bfloat16)
        for d in range(4):
            for j in range(4):
                outs[d][i + j] = tile(y, d, j, r, n)


def residual_kernel(start, sources, b_ref, bt_ref, phases_ref, observed_ref, *refs):
    outs, (angles, data, sems) = refs[-8:-4], refs[-3:]
    r, n = outs[0].shape[1:]
    copies = []
    for i in range(len(sources)):
        here, there = pl.ds(4 * i, 4), pl.ds(start + 4 * i, 4)
        copies.append(
            (
                pltpu.make_async_copy(phases_ref.at[:, there], angles.at[:, here], sems.at[0, i]),
                pltpu.make_async_copy(observed_ref.at[:, there], data.at[:, here], sems.at[1, i]),
            )
        )
        for copy in copies[-1]:
            copy.start()
    for i, (source, first) in enumerate(sources):
        ins = refs[4 * source : 4 * source + 4]
        x = stacked([[ref[first + j] for j in range(4)] for ref in ins])
        predicted = dot(b_ref[...], x)
        for copy in copies[i]:
            copy.wait()
        weighted = []
        for s in range(4):
            row = []
            for j in range(4):
                wave = cas(angles[s, 4 * i + j])
                residual = wave * tile(predicted, s, j, r, n)
                residual = residual - data[s, 4 * i + j].astype(jnp.float32)
                residual = residual.astype(jnp.bfloat16).astype(jnp.float32)
                row.append((wave * residual).astype(jnp.bfloat16))
            weighted.append(row)
        y = dot(bt_ref[...], stacked(weighted)).astype(jnp.bfloat16)
        for d in range(4):
            for j in range(4):
                outs[d][4 * i + j] = tile(y, d, j, r, n)


VMEM = pl.BlockSpec(memory_space=pltpu.VMEM)
ANY = pl.BlockSpec(memory_space=pl.ANY)
HBM = pl.BlockSpec(memory_space=pltpu.HBM)


KERNEL_COST = pl.CostEstimate(flops=0, bytes_accessed=0, transcendentals=0)
GATE_COST = pl.CostEstimate(flops=1000000000, bytes_accessed=1, transcendentals=0)


class Chain:
    def __init__(self, masks):
        self.token = None
        self.done = []
        count_x, count_y = lax.axis_size("qx"), lax.axis_size("qy")
        self.pairs = []
        for mask_x, mask_y in masks:
            along_y = [(s, s ^ mask_y) for s in range(count_y)]
            along_x = [(s, s ^ mask_x) for s in range(count_x)]
            both = [
                (x * count_y + y, (x ^ mask_x) * count_y + (y ^ mask_y))
                for x in range(count_x)
                for y in range(count_y)
            ]
            self.pairs.append((None, ("qy", along_y), ("qx", along_x), (("qx", "qy"), both)))

    def kernel(
        self, body, operands, specs, out_shapes, out_specs, aliases=None, gate=False, **options
    ):
        extra = [x for x in self.done if not any(x is y for y in operands)]
        self.done = []
        aliases = dict(aliases or {})
        token = [] if self.token is None else [self.token]
        if token:
            aliases[len(operands)] = len(out_shapes)
        outs = pl.pallas_call(
            body,
            out_shape=[*out_shapes, TOKEN],
            in_specs=[*specs, *[ANY] * (len(token) + len(extra))],
            out_specs=[*out_specs, ANY],
            input_output_aliases=aliases,
            compiler_params=pltpu.CompilerParams(vmem_limit_bytes=2**20 if gate else VMEM_GRANT),
            cost_estimate=GATE_COST if gate else KERNEL_COST,
            **options,
        )(*operands, *token, *extra)
        self.token = outs[-1]
        return outs[:-1]

    def send(self, block, level, d):
        shape = jax.ShapeDtypeStruct(block.shape, block.dtype)
        with jax.named_scope("gate_mark"):
            (block,) = self.kernel(gate_kernel, [block], [ANY], [shape], [ANY], {0: 0}, True)
        axis, pairs = self.pairs[level][d]
        return lax.ppermute(block, axis, pairs)


def local(image_tiles, observed, phases, interpolate, local_weights, merge_weights, output_weight):
    groups, r, n = image_tiles.shape[2:]
    depth = merge_weights.shape[2]
    chunks = len(X_PIECES)
    quarter = groups // 4
    chunk = quarter // chunks
    bf16 = jnp.bfloat16

    masks = []
    for level in range(depth):
        bit_x = level_bit(lax.axis_size("qx"), level, depth)
        bit_y = level_bit(lax.axis_size("qy"), level, depth)
        masks.append((2**bit_x, 2**bit_y))
    square = jax.ShapeDtypeStruct((4 * r, 4 * r), bf16)
    chain = Chain(masks)

    def pinned(x, shape):
        return pltpu.with_memory_space_constraint(x.reshape(shape), pltpu.HBM)

    image = pinned(image_tiles, (4, chunks, chunk, r, n))
    phase4 = pinned(phases, (4, quarter, r, n))
    observed4 = pinned(observed, (4, quarter, r, n))
    levels = pinned(local_weights, local_weights.shape[2:])
    inner = pinned(interpolate, interpolate.shape)

    def shapes(size):
        return [jax.ShapeDtypeStruct((size, r, n), bf16)] * 4

    def forward_local(index):
        sizes = X_PIECES[index]
        first = not prepared
        weights = [levels, inner] if first else list(prepared["local"])
        scratch = [pltpu.VMEM((4, chunk, r, n), bf16), pltpu.SemaphoreType.DMA((7,))]
        if first:
            scratch += [pltpu.VMEM(levels.shape, bf16), pltpu.VMEM((r, r), bf16)]
        outs_count = 4 * len(sizes) + 2 * first
        with jax.named_scope(f"local_forward_{index}"):
            outs = chain.kernel(
                functools.partial(forward_local_kernel, masks, sizes, index, first),
                [image, *weights],
                [HBM] + [HBM if first else VMEM] * 2,
                sum([shapes(size) for size in sizes], []) + [square] * (2 * first),
                [VMEM] * outs_count,
                scratch_shapes=scratch,
            )
        if first:
            prepared["local"] = outs[-2:]
        for piece in range(len(sizes)):
            ready["X0", x_first[index] + piece] = outs[4 * piece : 4 * piece + 4]

    def prepare_merges():
        with jax.named_scope("prep_merge"):
            prepared["merge"] = chain.kernel(
                functools.partial(prep_merge_kernel, masks),
                [merge_weights[0, 0], output_weight],
                [VMEM, VMEM],
                [square] * 4,
                [VMEM] * 4,
            )

    def prepare_adjoint():
        with jax.named_scope("prep_adjoint"):
            prepared["adjoint"] = chain.kernel(
                prep_adjoint_kernel,
                [local_weights[0, 0], interpolate],
                [VMEM, VMEM],
                [square] * 2,
                [VMEM] * 2,
            )

    def merge(weight, blocks):
        size = blocks[0].shape[0]
        return chain.kernel(
            merge_kernel,
            [weight, *blocks],
            [VMEM] * 5,
            shapes(size),
            [VMEM] * 4,
        )

    def through_data(number):
        start, size = y_starts[number], y_sizes[number]
        inside = [
            p for p, (a, m) in enumerate(zip(x_starts, x_sizes)) if a < start + size and start < a + m
        ]
        sources = []
        for box in range(start, start + size, 4):
            k = [i for i, p in enumerate(inside) if 0 <= box - x_starts[p] < x_sizes[p]][0]
            sources.append((k, box - x_starts[inside[k]]))
        blocks = sum([state["X1", p] for p in inside], [])
        return chain.kernel(
            functools.partial(residual_kernel, start, sources),
            [*prepared["merge"][2:], phase4, observed4, *blocks],
            [VMEM, VMEM, HBM, HBM] + [VMEM] * len(blocks),
            shapes(size),
            [VMEM] * 4,
            scratch_shapes=[
                pltpu.VMEM((4, size, r, n), jnp.float32),
                pltpu.VMEM((4, size, r, n), bf16),
                pltpu.SemaphoreType.DMA((2, size // 4)),
            ],
        )

    def adjoint_local(index):
        sizes = Y_PIECES[index]
        blocks = sum([state["Y0", y_first[index] + i] for i in range(len(sizes))], [])
        operands = [*prepared["adjoint"], *blocks]
        specs = [VMEM] * len(operands)
        aliases = {}
        if "gradient" in prepared:
            aliases = {len(operands): 0}
            operands.append(prepared["gradient"])
            specs.append(HBM)
        with jax.named_scope(f"local_adjoint_{index}"):
            (prepared["gradient"],) = chain.kernel(
                functools.partial(adjoint_local_kernel, masks, sizes, index),
                operands,
                specs,
                [jax.ShapeDtypeStruct((4, chunks, chunk, r, n), bf16)],
                [HBM],
                aliases,
                scratch_shapes=[
                    pltpu.VMEM((4, chunk, r, n), bf16),
                    pltpu.SemaphoreType.DMA((4,)),
                ],
            )

    x_sizes, y_sizes = sum(X_PIECES, ()), sum(Y_PIECES, ())
    x_starts = [sum(x_sizes[:i]) for i in range(len(x_sizes))]
    y_starts = [sum(y_sizes[:i]) for i in range(len(y_sizes))]
    x_first = [sum(len(p) for p in X_PIECES[:i]) for i in range(chunks)]
    y_first = [sum(len(p) for p in Y_PIECES[:i]) for i in range(chunks)]
    prepared, ready, state = {}, {}, {}

    for action in ACTIONS:
        mark, name, number = action[0], action[-4:-2], int(action[-2])
        if mark == ".":
            with jax.named_scope(f"{name}_{number}"):
                if name == "K1":
                    forward_local(number)
                elif name == "PM":
                    prepare_merges()
                elif name == "PA":
                    prepare_adjoint()
                elif name == "X1":
                    ready["X1", number] = merge(prepared["merge"][0], state["X0", number])
                elif name == "Y1":
                    ready["Y1", number] = through_data(number)
                elif name == "Y0":
                    ready["Y0", number] = merge(prepared["merge"][1], state["Y1", number])
                else:
                    adjoint_local(number)
            continue
        d = {"z": 1, "x": 2, "d": 3}[action[-1]]
        if mark == "+":
            blocks = ready[name, number]
            got = state.setdefault((name, number), [blocks[0], None, None, None])
            with jax.named_scope(f"{name}_{number}"):
                got[d] = chain.send(blocks[d], 1 if name in ("X1", "Y1") else 0, d)
        else:
            chain.done.append(state[name, number][d])
    return prepared["gradient"].reshape(1, 1, groups, r, n)


def solution(mesh):
    split = P("qx", "qy", None, None, None)
    weights = P("qx", "qy", None, None, None, None, None)
    return jax.shard_map(
        local,
        mesh=mesh,
        in_specs=(split, split, split, P(), weights, weights, P()),
        out_specs=split,
        check_vma=False,
    )
```

```python
import functools

import jax
import jax.numpy as jnp
import numpy as np
from jax import lax
from jax.experimental import pallas as pl
from jax.experimental.pallas import tpu as pltpu
from jax.sharding import PartitionSpec as P

X_PIECES = ((16,), (16,), (16,), (16,))
Y_PIECES = ((16,), (16,), (16,), (8, 8))
ACTIONS = (
    ".K10_", "+X00z", ".K13_", "+X03x", "+X00d", ".K11_", "+X01x", "+X00x", ".PM0_", ".K12_",
    "-X00z", "+X01d", "-X03x", "+X01z", "-X00d", "-X01x", "-X00x", ".X10_", "+X10d", "+X10x",
    "+X10z", "-X01d", "-X01z", ".X11_", "+X11x", "+X02d", "-X10d", "+X11z", "-X10x", "+X02x",
    ".PA0_", "-X10z", "+X02z", "-X11x", "+X11d", ".Y10_", "-X02d", "+Y10z", "-X11z", "+X03z",
    "-X02x", "+X03d", "-X02z", ".X12_", "+X12d", "-X11d", "+Y10x", ".Y11_", "-Y10z", "+X12z",
    "-X03z", "+Y11d", "-X03d", "+Y10d", "-X12d", "+Y11x", ".X13_", "-Y10x", "+X13z", "-X12z",
    "+X12x", "-Y11d", "+Y11z", "-Y10d", "+X13x", ".Y00_", "-Y11x", "+Y00d", "-X13z", "+X13d",
    "-X12x", "+Y00z", ".Y12_", "-Y11z", "+Y12x", "-X13x", "+Y12z", ".Y01_", "-Y00d", "+Y01d",
    "-X13d", ".Y13_", "+Y13x", "-Y00z", "+Y12d", "-Y12x", "+Y01z", ".Y14_", "-Y12z", "+Y01x",
    "-Y01d", "+Y14z", "-Y13x", "+Y14x", "-Y12d", ".Y02_", "+Y02d", "-Y01z", "+Y13z", "-Y01x",
    "+Y14d", "-Y14z", "+Y02z", "-Y14x", "+Y13d", ".K51_", "-Y02d", "-Y13z", "-Y14d", ".Y04_",
    "+Y04z", "+Y00x", "+Y02x", "-Y02z", "+Y04d", "-Y13d", ".Y03_", "+Y03d", "-Y04z", "+Y03z",
    "-Y00x", "+Y04x", "-Y02x", "+Y03x", ".K50_", ".K52_", "-Y04d", "-Y03d", "-Y04x", "-Y03z",
    "-Y03x", ".K53_",
)
VMEM_GRANT = 16 * 2**20
TOKEN = jax.ShapeDtypeStruct((8, 128), jnp.float32)
QUARTER_PI, HALF_PI = float(np.pi / 4), float(np.pi / 2)
SINE = (
    -1.4142135381698608,
    0.23570221662521362,
    -0.011785031296312809,
    0.00028053473215550184,
    -3.875064521707827e-06,
    3.182795182965492e-08,
)


def level_bit(axis_count, level_index, depth):
    total_bits = axis_count.bit_length() - 1
    return level_index * (total_bits - 1) // max(depth - 1, 1)


def dot(a, b):
    return jnp.dot(a, b, preferred_element_type=jnp.float32)


def cas(angle):
    rest = jnp.abs(angle - QUARTER_PI) - HALF_PI
    square = rest * rest
    poly = jnp.float32(SINE[-1])
    for c in SINE[-2::-1]:
        poly = poly * square + jnp.float32(c)
    return poly * rest


def stacked(columns):
    return jnp.concatenate([jnp.concatenate(row, axis=1) for row in columns], axis=0)


def tile(y, i, j, r, n):
    return y[i * r : (i + 1) * r, j * n : (j + 1) * n]


def own_index(masks):
    x, y = lax.axis_index("qx"), lax.axis_index("qy")
    return [
        2 * jnp.where(x & mask_x != 0, 1, 0) + jnp.where(y & mask_y != 0, 1, 0)
        for mask_x, mask_y in masks
    ]


def blocks_of(stack, r):
    return [
        jnp.concatenate([stack[4 * k + c] for c in range(4)], axis=1) for k in range(4)
    ]


def prep_adjoint_kernel(lw_ref, ip_ref, *refs):
    r = ip_ref.shape[0]
    w0t_ref, w1t_ref = refs[-3:-1]
    ip = ip_ref[...]
    for k in range(4):
        cols = pl.ds(k * r, r)
        for c in range(4):
            rows = pl.ds(c * r, r)
            w0t_ref[rows, cols] = dot(lw_ref[0, k, c], ip).T.astype(jnp.bfloat16)
            w1t_ref[rows, cols] = lw_ref[1, k, c].astype(jnp.float32).T.astype(jnp.bfloat16)


def prep_merge_kernel(masks, mw_ref, ow_ref, *refs):
    r = ow_ref.shape[0]
    a_ref, at_ref, b_ref, bt_ref = refs[-5:-1]
    ow = ow_ref[...]
    k0, k1 = own_index(masks)
    for s in range(4):
        rows = pl.ds(s * r, r)
        for c in range(4):
            cols = pl.ds(c * r, r)
            a = mw_ref[0, k1 ^ s, k0 ^ c]
            b = dot(ow, mw_ref[1, s, k1 ^ c])
            a_ref[rows, cols] = a
            at_ref[cols, rows] = a.astype(jnp.float32).T.astype(jnp.bfloat16)
            b_ref[rows, cols] = b.astype(jnp.bfloat16)
            bt_ref[cols, rows] = b.T.astype(jnp.bfloat16)


def gate_kernel(*refs):
    pass


def forward_local_kernel(masks, sizes, index, first, *refs):
    image_ref, first_ref, second_ref = refs[:3]
    refs, (tiles, sems, *held) = (refs[:-4], refs[-4:]) if first else (refs[:-2], refs[-2:])
    copies = []
    k0 = own_index(masks)[0]
    for i, (source, target) in enumerate(zip((first_ref, second_ref), held)):
        copies.append(pltpu.make_async_copy(source, target, sems.at[4 + i]))
    for d in range(4):
        copies.append(
            pltpu.make_async_copy(image_ref.at[k0 ^ d, index], tiles.at[d], sems.at[d])
        )
    for copy in copies:
        copy.start()
    if first:
        w0_ref, w1_ref = refs[-3:-1]
        outs = refs[-3 - 4 * len(sizes) : -3]
        levels, inner = held
        r = inner.shape[0]
        for copy in copies[:2]:
            copy.wait()
        copies = copies[2:]
        folded = dot(levels[0].reshape(16 * r, r), inner[...]).astype(jnp.bfloat16)
        w0 = jnp.concatenate(blocks_of(folded.reshape(16, r, r), r), axis=0)
        w1 = jnp.concatenate(blocks_of(levels[1].reshape(16, r, r), r), axis=0)
        w0_ref[...], w1_ref[...] = w0, w1
    else:
        w0, w1 = first_ref[...], second_ref[...]
        outs = refs[-1 - 4 * len(sizes) : -1]
    r, n = tiles.shape[-2:]
    for d in range(4):
        copies[d].wait()
        x = stacked([[tiles[d, 4 * a + c] for a in range(4)] for c in range(4)])
        y = dot(w0, x).astype(jnp.bfloat16)
        x = stacked([[tile(y, e, a, r, n) for e in range(4)] for a in range(4)])
        y = dot(w1, x).astype(jnp.bfloat16)
        start = 0
        for piece, size in enumerate(sizes):
            for h in range(size):
                a, e = divmod(start + h, 4)
                outs[4 * piece + d][h] = tile(y, a, e, r, n)
            start += size


def adjoint_local_kernel(masks, sizes, index, w0t_ref, w1t_ref, *refs):
    ins, out_ref, tiles, sems = refs[: 4 * len(sizes)], refs[-4], refs[-2], refs[-1]
    r, n = tiles.shape[-2:]
    w0t, w1t = w0t_ref[...], w1t_ref[...]
    places = [(piece, h) for piece, size in enumerate(sizes) for h in range(size)]
    k0 = own_index(masks)[0]
    copies = []
    for d in range(4):

        def piece_of(a, e):
            piece, h = places[4 * a + e]
            return ins[4 * piece + d][h]

        x = stacked([[piece_of(a, e) for e in range(4)] for a in range(4)])
        y = dot(w1t, x).astype(jnp.bfloat16)
        x = stacked([[tile(y, a, e, r, n) for a in range(4)] for e in range(4)])
        y = dot(w0t, x).astype(jnp.bfloat16)
        for a in range(4):
            for c in range(4):
                tiles[d, 4 * a + c] = tile(y, c, a, r, n)
        copies.append(
            pltpu.make_async_copy(tiles.at[d], out_ref.at[k0 ^ d, index], sems.at[d])
        )
        copies[-1].start()
    for copy in copies:
        copy.wait()


def merge_kernel(w_ref, *refs):
    ins, outs = refs[:4], refs[-5:-1]
    size, r, n = ins[0].shape
    w = w_ref[...]
    for i in range(0, size, 4):
        x = stacked([[ref[i + j] for j in range(4)] for ref in ins])
        y = dot(w, x).astype(jnp.bfloat16)
        for d in range(4):
            for j in range(4):
                outs[d][i + j] = tile(y, d, j, r, n)


def residual_kernel(start, sources, b_ref, bt_ref, phases_ref, observed_ref, *refs):
    outs, (angles, data, sems) = refs[-8:-4], refs[-3:]
    r, n = outs[0].shape[1:]
    copies = []
    for i in range(len(sources)):
        here, there = pl.ds(4 * i, 4), pl.ds(start + 4 * i, 4)
        copies.append(
            (
                pltpu.make_async_copy(phases_ref.at[:, there], angles.at[:, here], sems.at[0, i]),
                pltpu.make_async_copy(observed_ref.at[:, there], data.at[:, here], sems.at[1, i]),
            )
        )
        for copy in copies[-1]:
            copy.start()
    for i, (source, first) in enumerate(sources):
        ins = refs[4 * source : 4 * source + 4]
        x = stacked([[ref[first + j] for j in range(4)] for ref in ins])
        predicted = dot(b_ref[...], x)
        for copy in copies[i]:
            copy.wait()
        weighted = []
        for s in range(4):
            row = []
            for j in range(4):
                wave = cas(angles[s, 4 * i + j])
                residual = wave * tile(predicted, s, j, r, n)
                residual = residual - data[s, 4 * i + j].astype(jnp.float32)
                residual = residual.astype(jnp.bfloat16).astype(jnp.float32)
                row.append((wave * residual).astype(jnp.bfloat16))
            weighted.append(row)
        y = dot(bt_ref[...], stacked(weighted)).astype(jnp.bfloat16)
        for d in range(4):
            for j in range(4):
                outs[d][4 * i + j] = tile(y, d, j, r, n)


VMEM = pl.BlockSpec(memory_space=pltpu.VMEM)
ANY = pl.BlockSpec(memory_space=pl.ANY)
HBM = pl.BlockSpec(memory_space=pltpu.HBM)


KERNEL_COST = pl.CostEstimate(flops=0, bytes_accessed=0, transcendentals=0)
GATE_COST = pl.CostEstimate(flops=1000000000, bytes_accessed=1, transcendentals=0)


class Chain:
    def __init__(self, masks):
        self.token = None
        self.done = []
        count_x, count_y = lax.axis_size("qx"), lax.axis_size("qy")
        self.pairs = []
        for mask_x, mask_y in masks:
            along_y = [(s, s ^ mask_y) for s in range(count_y)]
            along_x = [(s, s ^ mask_x) for s in range(count_x)]
            both = [
                (x * count_y + y, (x ^ mask_x) * count_y + (y ^ mask_y))
                for x in range(count_x)
                for y in range(count_y)
            ]
            self.pairs.append((None, ("qy", along_y), ("qx", along_x), (("qx", "qy"), both)))

    def kernel(
        self, body, operands, specs, out_shapes, out_specs, aliases=None, gate=False, **options
    ):
        extra = [x for x in self.done if not any(x is y for y in operands)]
        self.done = []
        aliases = dict(aliases or {})
        token = [] if self.token is None else [self.token]
        if token:
            aliases[len(operands)] = len(out_shapes)
        outs = pl.pallas_call(
            body,
            out_shape=[*out_shapes, TOKEN],
            in_specs=[*specs, *[ANY] * (len(token) + len(extra))],
            out_specs=[*out_specs, ANY],
            input_output_aliases=aliases,
            compiler_params=pltpu.CompilerParams(vmem_limit_bytes=2**20 if gate else VMEM_GRANT),
            cost_estimate=GATE_COST if gate else KERNEL_COST,
            **options,
        )(*operands, *token, *extra)
        self.token = outs[-1]
        return outs[:-1]

    def send(self, block, level, d):
        shape = jax.ShapeDtypeStruct(block.shape, block.dtype)
        with jax.named_scope("gate_mark"):
            (block,) = self.kernel(gate_kernel, [block], [ANY], [shape], [ANY], {0: 0}, True)
        axis, pairs = self.pairs[level][d]
        return lax.ppermute(block, axis, pairs)


def local(image_tiles, observed, phases, interpolate, local_weights, merge_weights, output_weight):
    groups, r, n = image_tiles.shape[2:]
    depth = merge_weights.shape[2]
    chunks = len(X_PIECES)
    quarter = groups // 4
    chunk = quarter // chunks
    bf16 = jnp.bfloat16

    masks = []
    for level in range(depth):
        bit_x = level_bit(lax.axis_size("qx"), level, depth)
        bit_y = level_bit(lax.axis_size("qy"), level, depth)
        masks.append((2**bit_x, 2**bit_y))
    square = jax.ShapeDtypeStruct((4 * r, 4 * r), bf16)
    chain = Chain(masks)

    def pinned(x, shape):
        return pltpu.with_memory_space_constraint(x.reshape(shape), pltpu.HBM)

    image = pinned(image_tiles, (4, chunks, chunk, r, n))
    phase4 = pinned(phases, (4, quarter, r, n))
    observed4 = pinned(observed, (4, quarter, r, n))
    levels = pinned(local_weights, local_weights.shape[2:])
    inner = pinned(interpolate, interpolate.shape)

    def shapes(size):
        return [jax.ShapeDtypeStruct((size, r, n), bf16)] * 4

    def forward_local(index):
        sizes = X_PIECES[index]
        first = not prepared
        weights = [levels, inner] if first else list(prepared["local"])
        scratch = [pltpu.VMEM((4, chunk, r, n), bf16), pltpu.SemaphoreType.DMA((6,))]
        if first:
            scratch += [pltpu.VMEM(levels.shape, bf16), pltpu.VMEM((r, r), bf16)]
        outs_count = 4 * len(sizes) + 2 * first
        with jax.named_scope(f"local_forward_{index}"):
            outs = chain.kernel(
                functools.partial(forward_local_kernel, masks, sizes, index, first),
                [image, *weights],
                [HBM] + [HBM if first else VMEM] * 2,
                sum([shapes(size) for size in sizes], []) + [square] * (2 * first),
                [VMEM] * outs_count,
                scratch_shapes=scratch,
            )
        if first:
            prepared["local"] = outs[-2:]
        for piece in range(len(sizes)):
            ready["X0", x_first[index] + piece] = outs[4 * piece : 4 * piece + 4]

    def prepare_merges():
        with jax.named_scope("prep_merge"):
            prepared["merge"] = chain.kernel(
                functools.partial(prep_merge_kernel, masks),
                [merge_weights[0, 0], output_weight],
                [VMEM, VMEM],
                [square] * 4,
                [VMEM] * 4,
            )

    def prepare_adjoint():
        with jax.named_scope("prep_adjoint"):
            prepared["adjoint"] = chain.kernel(
                prep_adjoint_kernel,
                [local_weights[0, 0], interpolate],
                [VMEM, VMEM],
                [square] * 2,
                [VMEM] * 2,
            )

    def merge(weight, blocks):
        size = blocks[0].shape[0]
        return chain.kernel(
            merge_kernel,
            [weight, *blocks],
            [VMEM] * 5,
            shapes(size),
            [VMEM] * 4,
        )

    def through_data(number):
        start, size = y_starts[number], y_sizes[number]
        inside = [
            p for p, (a, m) in enumerate(zip(x_starts, x_sizes)) if a < start + size and start < a + m
        ]
        sources = []
        for box in range(start, start + size, 4):
            k = [i for i, p in enumerate(inside) if 0 <= box - x_starts[p] < x_sizes[p]][0]
            sources.append((k, box - x_starts[inside[k]]))
        blocks = sum([state["X1", p] for p in inside], [])
        return chain.kernel(
            functools.partial(residual_kernel, start, sources),
            [*prepared["merge"][2:], phase4, observed4, *blocks],
            [VMEM, VMEM, HBM, HBM] + [VMEM] * len(blocks),
            shapes(size),
            [VMEM] * 4,
            scratch_shapes=[
                pltpu.VMEM((4, size, r, n), jnp.float32),
                pltpu.VMEM((4, size, r, n), bf16),
                pltpu.SemaphoreType.DMA((2, size // 4)),
            ],
        )

    def adjoint_local(index):
        sizes = Y_PIECES[index]
        blocks = sum([state["Y0", y_first[index] + i] for i in range(len(sizes))], [])
        operands = [*prepared["adjoint"], *blocks]
        specs = [VMEM] * len(operands)
        aliases = {}
        if "gradient" in prepared:
            aliases = {len(operands): 0}
            operands.append(prepared["gradient"])
            specs.append(HBM)
        with jax.named_scope(f"local_adjoint_{index}"):
            (prepared["gradient"],) = chain.kernel(
                functools.partial(adjoint_local_kernel, masks, sizes, index),
                operands,
                specs,
                [jax.ShapeDtypeStruct((4, chunks, chunk, r, n), bf16)],
                [HBM],
                aliases,
                scratch_shapes=[
                    pltpu.VMEM((4, chunk, r, n), bf16),
                    pltpu.SemaphoreType.DMA((4,)),
                ],
            )

    x_sizes, y_sizes = sum(X_PIECES, ()), sum(Y_PIECES, ())
    x_starts = [sum(x_sizes[:i]) for i in range(len(x_sizes))]
    y_starts = [sum(y_sizes[:i]) for i in range(len(y_sizes))]
    x_first = [sum(len(p) for p in X_PIECES[:i]) for i in range(chunks)]
    y_first = [sum(len(p) for p in Y_PIECES[:i]) for i in range(chunks)]
    prepared, ready, state = {}, {}, {}

    for action in ACTIONS:
        mark, name, number = action[0], action[-4:-2], int(action[-2])
        if mark == ".":
            with jax.named_scope(f"{name}_{number}"):
                if name == "K1":
                    forward_local(number)
                elif name == "PM":
                    prepare_merges()
                elif name == "PA":
                    prepare_adjoint()
                elif name == "X1":
                    ready["X1", number] = merge(prepared["merge"][0], state["X0", number])
                elif name == "Y1":
                    ready["Y1", number] = through_data(number)
                elif name == "Y0":
                    ready["Y0", number] = merge(prepared["merge"][1], state["Y1", number])
                else:
                    adjoint_local(number)
            continue
        d = {"z": 1, "x": 2, "d": 3}[action[-1]]
        if mark == "+":
            blocks = ready[name, number]
            got = state.setdefault((name, number), [blocks[0], None, None, None])
            with jax.named_scope(f"{name}_{number}"):
                got[d] = chain.send(blocks[d], 1 if name in ("X1", "Y1") else 0, d)
        else:
            chain.done.append(state[name, number][d])
    return prepared["gradient"].reshape(1, 1, groups, r, n)


def solution(mesh):
    split = P("qx", "qy", None, None, None)
    weights = P("qx", "qy", None, None, None, None, None)
    return jax.shard_map(
        local,
        mesh=mesh,
        in_specs=(split, split, split, P(), weights, weights, P()),
        out_specs=split,
        check_vma=False,
    )
```
